32 devices in a mesh: groups: 2 (over x), ctx: 16 (over z, y, core).
Axes of the slice: x: 2, y: 2, z: 4, core: 2. Of those that a mesh axis runs over, the one named last changes fastest.
Arguments:
- q_raw: bfloat16 [16384, 1024], P(('groups', 'ctx')), parts along dimension 0, may hold values from -6 to 6
- k_raw: bfloat16 [16384, 1024], P(('groups', 'ctx')), parts along dimension 0, may hold values from -6 to 6
- v_raw: bfloat16 [16384, 2048], P(('groups', 'ctx')), parts along dimension 0, may hold values from -6 to 6
- conv_weight: float32 [4, 4096], replicated, may hold values from -3 to 3
- gate_log: float32 [16384, 16], P(('groups', 'ctx')), parts along dimension 0, may hold values from -1 to 0
- beta: float32 [16384, 16], P(('groups', 'ctx')), parts along dimension 0, may hold values from 0 to 0.9
- gate_z: bfloat16 [16384, 2048], P(('groups', 'ctx')), parts along dimension 0, may hold values from -6 to 6
- norm_gain: float32 [128], replicated, may hold values from 0.1 to 1.9
- doc_start: int32 [32], P(('groups', 'ctx')), parts along dimension 0, may hold values from 0 to 512, as said below
Outputs:
- mixed: bfloat16 [16384, 2048], P(('groups', 'ctx')), parts along dimension 0
The draws below stay inside these ranges and needn't reach their ends.
There are 2 independent parts, one for each index of `groups`. The reference program is written for one: setup_inputs(seed, part) draws one part's arguments, and reference() takes and returns one part's arrays. A program takes and returns all parts, laid end to end along the dimension named above; an argument that names none is the same for every part. Nothing has to cross between parts.
Inputs may be any that keep to these rules, and one draw needn't show every extreme that they name: `doc_start`: at most one document begins in a slab; the value is 512 where none begins.
All inputs are finite; a program needn't handle non-finite values.
Results may differ from the reference program's by a relative error of at most 0.0045.
Values may be sent and summed in bfloat16 or wider, within the bound.
A program may use at most 128 MiB of HBM per device.

```python
import math
import jax
import jax.numpy as jnp
from jax import lax

HK = 8
HV = 16
DK = 128
DV = 128
KCONV = 4
SPAN = 64
SLAB = 512
SEQUENCE_LENGTH = 8192


def forgetting_speed_layout(key, lagging_share):
    slab_count = SEQUENCE_LENGTH // SLAB
    first_key, second_key, sampler_seed_triple = jax.random.split(key, 3)
    lagging_attention_units = (jax.random.uniform(first_key, (HV,)) < lagging_share).astype(jnp.float32)
    speed_variation = jnp.exp(jax.random.uniform(second_key, (slab_count, 1, HV), minval=math.log(0.5), maxval=math.log(2.0)))
    speed_variation = jnp.broadcast_to(speed_variation, (slab_count, SLAB, HV)).reshape(SEQUENCE_LENGTH, HV)
    spike_locations = jax.random.randint(sampler_seed_triple, (2,), 0, SEQUENCE_LENGTH)
    spike_amounts = jnp.any(jnp.arange(SEQUENCE_LENGTH)[:, None] == spike_locations[None, :], axis=1).astype(jnp.float32)
    return (lagging_attention_units, speed_variation, spike_amounts)


def draw_gate_log(key, part):
    lagging_share = 0.5
    lagging_attention_units, speed_variation, spike_amounts = forgetting_speed_layout(key, lagging_share)
    key = jax.random.fold_in(key, 11)
    rough_key, drop_key = jax.random.split(key)
    forget_jitter_level = jax.random.uniform(rough_key, (SEQUENCE_LENGTH, HV), minval=0.5, maxval=1.5)
    fast_rate = math.log(10.0) / 40.0
    slow_rate = 0.1 * math.log(10.0) / SEQUENCE_LENGTH
    forgetting_speeds = lagging_attention_units * slow_rate + (1.0 - lagging_attention_units) * fast_rate
    forgetting_falls = jnp.log(jax.random.uniform(drop_key, (SEQUENCE_LENGTH, HV), minval=0.5, maxval=0.8))
    return (-forgetting_speeds[None, :] * speed_variation * forget_jitter_level + spike_amounts[:, None] * forgetting_falls).astype(jnp.float32)


def draw_beta(key, part):
    lagging_share = 0.5
    lagging_attention_units, speed_variation, spike_amounts = forgetting_speed_layout(key, lagging_share)
    key = jax.random.fold_in(key, 23)
    fast_key, slow_key = jax.random.split(key)
    fast_values = jax.random.uniform(fast_key, (SEQUENCE_LENGTH, HV), minval=0.2, maxval=0.9)
    slow_values = DK / SEQUENCE_LENGTH * jax.random.uniform(slow_key, (SEQUENCE_LENGTH, HV), minval=0.5, maxval=1.5)
    return (lagging_attention_units[None, :] * slow_values + (1.0 - lagging_attention_units[None, :]) * fast_values).astype(jnp.float32)


def draw_doc_start(key, part):
    key = jax.random.fold_in(key, 5)
    key = jax.random.fold_in(key, part)
    slab_count = SEQUENCE_LENGTH // SLAB
    pick_key, place_key = jax.random.split(key)
    reset_count = max(2, slab_count // 32)
    chosen = jax.random.permutation(pick_key, slab_count)[:reset_count]
    slab_index = jnp.arange(slab_count)
    marked = jnp.any(slab_index[:, None] == chosen[None, :], axis=1)
    offsets = jax.random.randint(place_key, (slab_count,), 0, SLAB)
    offsets = jnp.where(slab_index == chosen[0], 0, offsets)
    return jnp.where(marked, offsets, SLAB).astype(jnp.int32)


def block_scale(rng, extent, cuts, low, high):
    def one(axis_at, blocks):
        draws = jax.random.uniform(jax.random.fold_in(jax.random.fold_in(rng, 6), axis_at), (blocks,), jnp.float32, low / len(cuts), high / len(cuts))
        return jnp.repeat(jnp.exp(draws), extent[axis_at] // blocks).reshape((-1,) + (1,) * (len(extent) - axis_at - 1))

    gain = one(*cuts[0])
    for cut in cuts[1:]:
        gain = gain * one(*cut)
    return gain


def noise(key, extent, width, bound, pieces=(), kind=jnp.bfloat16):
    values = jax.random.normal(key, extent, jnp.float32) * width
    if len(pieces) > 0:
        values = block_scale(key, extent, pieces, -0.22, 0.18) * values
    return jnp.clip(values, min=-bound, max=bound).astype(kind)


def setup_inputs(seed: int = 0, part: int = 0) -> dict:
    streams_of = jax.random.split(jax.random.key(seed), 10)
    own_keys = jax.random.split(jax.random.fold_in(streams_of[9], part), 10)
    q_raw = noise(own_keys[0], (SEQUENCE_LENGTH, HK * DK), 1.0, 6.0, ((0, 16),))
    k_raw = noise(own_keys[1], (SEQUENCE_LENGTH, HK * DK), 1.0, 6.0, ((0, 16),))
    v_raw = noise(own_keys[2], (SEQUENCE_LENGTH, HV * DV), 1.0, 6.0, ((0, 16),))
    conv_weight = noise(streams_of[3], (KCONV, 2 * HK * DK + HV * DV), KCONV ** -0.5, 3.0, (), jnp.float32)
    gate_log = draw_gate_log(jax.random.fold_in(jax.random.fold_in(streams_of[9], part), 71), part)
    beta = draw_beta(jax.random.fold_in(jax.random.fold_in(streams_of[9], part), 71), part)
    gate_z = noise(own_keys[6], (SEQUENCE_LENGTH, HV * DV), 1.0, 6.0, ((0, 16),))
    norm_gain = jnp.clip(1.0 + 0.18 * jax.random.normal(streams_of[7], (DV,), jnp.float32), 0.1, 1.9)
    doc_start = draw_doc_start(jax.random.fold_in(jax.random.fold_in(streams_of[9], part), 71), part)
    return dict(q_raw=q_raw, k_raw=k_raw, v_raw=v_raw, conv_weight=conv_weight, gate_log=gate_log, beta=beta, gate_z=gate_z, norm_gain=norm_gain, doc_start=doc_start)


precise = lax.Precision.HIGHEST

def conv_silu(raw_block, rim_rows, block_docs, rim_docs, weights):
    extended = jnp.concatenate([rim_rows, raw_block], axis=0)
    extended_docs = jnp.concatenate([rim_docs, block_docs], axis=0)
    length = raw_block.shape[0]
    summed = jnp.zeros(raw_block.shape, jnp.float32)
    for offset in range(weights.shape[0]):
        window = extended[offset:offset + length].astype(jnp.float32)
        usable = (extended_docs[offset:offset + length] == block_docs)[:, None]
        summed = summed + jnp.where(usable, weights[offset][None, :] * window, 0.0)
    return jax.nn.silu(summed).astype(jnp.bfloat16)

def unit_rows(values, head_count, factor):
    shaped = values.astype(jnp.float32).reshape(values.shape[0], head_count, -1)
    return shaped / jnp.sqrt(lax.optimization_barrier(jnp.sum(shaped * shaped, axis=-1, keepdims=True)) + 1e-06) * factor

def unit_lower_inverse(lower_part):
    length = lower_part.shape[-1]
    eye_rows = jnp.eye(length, dtype=jnp.float32)[None]
    power = -lower_part
    inverse = eye_rows + power
    for step in range((length - 1).bit_length() - 1):
        power = jnp.einsum('hij,hjk->hik', power, power, precision=precise)
        inverse = jnp.einsum('hij,hjk->hik', inverse, eye_rows + power, precision=precise)
    return inverse

def block_terms(query_conv, key_conv, value_conv, gate_block, beta_block, block_docs, prior_doc):
    length = query_conv.shape[0]
    queries = jnp.repeat(unit_rows(query_conv, HK, DK ** (-0.5)), HV // HK, axis=1)
    key_rows = jnp.repeat(unit_rows(key_conv, HK, 1.0), HV // HK, axis=1)
    values = value_conv.astype(jnp.float32).reshape(length, HV, DV)
    cumulative = jnp.cumsum(gate_block, axis=0)
    places = jnp.arange(length)
    same_doc = block_docs[:, None] == block_docs[None, :]
    within = (places[:, None] >= places[None, :]) & same_doc
    strictly = (places[:, None] > places[None, :]) & same_doc
    heads_first = cumulative.T
    spread_log = heads_first[:, :, None] - heads_first[:, None, :]
    decay_incl = jnp.exp(jnp.where(within[None], spread_log, -jnp.inf))
    decay_strict = jnp.where(strictly[None], decay_incl, 0.0)
    key_gram = jnp.einsum('ihd,jhd->hij', key_rows, key_rows, precision=precise)
    lower_part = beta_block.T[:, :, None] * key_gram * decay_strict
    start_open = (block_docs == prior_doc).astype(jnp.float32)
    end_open = (block_docs == block_docs[-1]).astype(jnp.float32)
    carries = (block_docs[-1] == prior_doc).astype(jnp.float32)
    growth = jnp.exp(cumulative)
    weight_in = (beta_block * growth * start_open[:, None])[:, :, None] * key_rows
    value_in = beta_block[:, :, None] * values
    stacked = jnp.concatenate([weight_in, value_in], axis=-1).transpose(1, 0, 2)
    solved = jnp.einsum('hij,hjd->hid', unit_lower_inverse(lower_part), stacked, precision=precise)
    key_width = key_rows.shape[-1]
    weight_rows = solved[:, :, :key_width]
    pseudo_values = solved[:, :, key_width:]
    attend = jnp.einsum('ihd,jhd->hij', queries, key_rows, precision=precise) * decay_incl
    query_decayed = ((growth * start_open[:, None])[:, :, None] * queries).transpose(1, 0, 2)
    tail_decay = jnp.exp(cumulative[-1][None, :] - cumulative) * end_open[:, None]
    key_decayed = (tail_decay[:, :, None] * key_rows).transpose(1, 0, 2)
    block_decay = jnp.exp(cumulative[-1]) * carries
    return (weight_rows, pseudo_values, attend, query_decayed, key_decayed, block_decay)

def gated_norm(outputs, gate_rows, gain_row):
    mean_square = lax.optimization_barrier(jnp.mean(outputs * outputs, axis=-1, keepdims=True))
    normed = outputs * lax.rsqrt(mean_square + 1e-06) * gain_row
    gate_values = gate_rows.astype(jnp.float32).reshape(outputs.shape)
    return (normed * jax.nn.silu(gate_values)).astype(jnp.bfloat16).reshape(outputs.shape[0], -1)

def reference(q_raw, k_raw, v_raw, conv_weight, gate_log, beta, gate_z, norm_gain, doc_start):
    has_start = (doc_start < SLAB).astype(jnp.int32)
    earlier = jnp.cumsum(has_start) - has_start
    places = jnp.arange(SLAB, dtype=jnp.int32)
    doc_ids = (earlier[:, None] + (places[None, :] >= doc_start[:, None]).astype(jnp.int32)).reshape(SEQUENCE_LENGTH)
    q_width = HK * DK
    conv_query = conv_weight[:, :q_width]
    conv_key = conv_weight[:, q_width:2 * q_width]
    conv_value = conv_weight[:, 2 * q_width:]
    blocks = SEQUENCE_LENGTH // SPAN
    margin = KCONV - 1

    def advance(chain_carry, inputs):
        rim_query, rim_key, rim_value, rim_docs, memory = chain_carry
        raw_query, raw_key, raw_value, gate_block, beta_block, gate_rows, block_docs = inputs
        query_conv = conv_silu(raw_query, rim_query, block_docs, rim_docs, conv_query)
        key_conv = conv_silu(raw_key, rim_key, block_docs, rim_docs, conv_key)
        value_conv = conv_silu(raw_value, rim_value, block_docs, rim_docs, conv_value)
        terms = block_terms(query_conv, key_conv, value_conv, gate_block, beta_block, block_docs, rim_docs[-1])
        weight_rows, pseudo_values, attend, query_decayed, key_decayed, block_decay = terms
        fresh_rows = pseudo_values - jnp.einsum('hck,hvk->hcv', weight_rows, memory, precision=precise)
        outputs = jnp.einsum('hck,hvk->chv', query_decayed, memory, precision=precise)
        outputs = outputs + jnp.einsum('hij,hjv->ihv', attend, fresh_rows, precision=precise)
        memory = block_decay[:, None, None] * memory + jnp.einsum('hcv,hck->hvk', fresh_rows, key_decayed, precision=precise)
        result_rows = gated_norm(outputs, gate_rows, norm_gain)
        new_carry = (raw_query[SPAN - margin:], raw_key[SPAN - margin:], raw_value[SPAN - margin:], block_docs[SPAN - margin:], memory)
        return (new_carry, result_rows)
    initial = (jnp.zeros((margin, q_width), jnp.bfloat16), jnp.zeros((margin, q_width), jnp.bfloat16), jnp.zeros((margin, HV * DV), jnp.bfloat16), jnp.full((margin,), -1, jnp.int32), jnp.zeros((HV, DV, DK), jnp.float32))
    inputs = (q_raw.reshape(blocks, SPAN, q_width), k_raw.reshape(blocks, SPAN, q_width), v_raw.reshape(blocks, SPAN, HV * DV), gate_log.reshape(blocks, SPAN, HV), beta.reshape(blocks, SPAN, HV), gate_z.reshape(blocks, SPAN, HV * DV), doc_ids.reshape(blocks, SPAN))
    _, result_rows = lax.scan(advance, initial, inputs)
    return result_rows.reshape(SEQUENCE_LENGTH, HV * DV)
```

```python
import functools

import jax
import jax.numpy as jnp
from jax import lax
from jax.experimental import pallas as pl
from jax.experimental.pallas import tpu as pltpu
from jax.sharding import PartitionSpec as P

HK = 8
HV = 16
DK = 128
DV = 128
CH = 128
RIM = 16
f32 = jnp.float32
bf16 = jnp.bfloat16


def split(x):
    hi = x.astype(bf16)
    return hi, (x - hi.astype(f32)).astype(bf16)


def mm(a, b):
    return lax.dot_general(a, b, (((1,), (0,)), ((), ())), preferred_element_type=f32)


def mm_nt(a, b):
    return lax.dot_general(a, b, (((1,), (1,)), ((), ())), preferred_element_type=f32)


def nt3(a, b):
    ah, al = split(a)
    bh, bl = split(b)
    return mm_nt(ah, bh) + mm_nt(al, bh) + mm_nt(ah, bl)


def mm3(ah, al, bh, bl):
    left = jnp.concatenate([ah, al], axis=1)
    return mm(left, jnp.concatenate([bh, bh], axis=0)) + mm(ah, bl)


def conv(ext, raw, rim, w, since, length):
    width = raw.shape[1]
    ext[0:RIM, 0:width] = rim.astype(f32)
    ext[RIM : RIM + length, 0:width] = raw.astype(f32)
    taps = w.shape[0]
    total = None
    for s in range(taps):
        back = taps - 1 - s
        term = ext[RIM - back : RIM - back + length, 0:width] * w[s : s + 1, :]
        if back:
            term = jnp.where(since < back, 0.0, term)
        total = term if total is None else total + term
    return (total / (1.0 + jnp.exp(-total))).astype(bf16)


def slab_kernel(
    doc, q, k, v, rq, rk, rv, wq, wk, wv, cumc, cumr, betac, betar, loc, reach, smap, soff, ext
):
    length = q.shape[0]
    sd = doc[0]
    row = lax.broadcasted_iota(jnp.int32, (length, DK), 0) - sd
    since = jnp.where(row < 0, length + 8, row)
    qc = conv(ext, q[...], rq[...], wq[...], since, length)
    kc = conv(ext, k[...], rk[...], wk[...], since, length)
    since2 = jnp.concatenate([since, since], axis=1)
    vc = conv(ext, v[...], rv[...], wv[...], since2, length)
    chunks = length // CH
    ii = lax.broadcasted_iota(jnp.int32, (CH, CH), 0)
    jj = lax.broadcasted_iota(jnp.int32, (CH, CH), 1)
    ix = ii ^ jj
    eye = ii == jj
    eyef = jnp.where(eye, 1.0, 0.0)
    tcol = lax.broadcasted_iota(jnp.int32, (CH, 1), 0)
    shared = []
    lowers = []
    per = []
    for c in range(chunks):
        b = c * CH
        kcc, qcc = kc[b : b + CH], qc[b : b + CH]
        kq = jnp.concatenate([kcc, qcc], axis=0)
        gram = mm_nt(kq, kcc)
        kk = jnp.where(eye, gram[:CH], 0.0)
        k_row = lax.rsqrt(jnp.sum(kk, axis=0, keepdims=True) + 1e-6)
        k_col = lax.rsqrt(jnp.sum(kk, axis=1, keepdims=True) + 1e-6)
        qf = qcc.astype(f32)
        q_col = lax.rsqrt(jnp.sum(qf * qf, axis=1, keepdims=True) + 1e-6) * (DK**-0.5)
        same = (ii + b >= sd) == (jj + b >= sd)
        mask = jnp.where((ii >= jj) & same, 0.0, -1e30)
        gs = gram[:CH] * k_col * k_row
        ats = gram[CH:] * q_col * k_row
        opened = jnp.where((tcol + b >= sd) & (b - 1 < sd), 0.0, 1.0)
        ended = jnp.where((tcol + b < sd) & (b + CH - 1 >= sd), 0.0, 1.0)
        carries = jnp.where((b + CH - 1 >= sd) & (b - 1 < sd), 0.0, 1.0)
        kt = kcc.astype(f32).T.astype(bf16)
        shared.append((jnp.concatenate([kq, kq], axis=1), jnp.concatenate([kt, kt], axis=1)))
        for e in range(2):
            cc = cumc[0, b : b + CH, e : e + 1]
            cr = cumr[0, e : e + 1, b : b + CH]
            bc = betac[0, b : b + CH, e : e + 1]
            br = betar[0, e : e + 1, b : b + CH]
            decay = jnp.exp(cc - cr + mask)
            lower = gs * decay * bc
            att = ats * decay
            growth = jnp.exp(cc) * opened
            last = cc[CH - 1 : CH]
            tail = jnp.exp(last - cc) * ended * k_col
            lowers.append(lower)
            per.append(
                (
                    jnp.concatenate(split(att), axis=1),
                    growth * k_col,
                    growth * q_col,
                    tail,
                    jnp.exp(last) * carries,
                    br,
                )
            )
    count = len(lowers)
    inv = [eyef - jnp.where(ix == 1, lw, 0.0) for lw in lowers]
    lsp = [split(lw) for lw in lowers]
    for lm in range(1, (CH - 1).bit_length()):
        pick = (ix >> lm) == 1
        zero = jnp.zeros((CH, CH), bf16)
        tsp = [split(t) for t in inv]
        low = [(jnp.where(pick, a, zero), jnp.where(pick, d, zero)) for a, d in lsp]
        es = [mm3(*low[n], *tsp[n]) for n in range(count)]
        esp = [split(x) for x in es]
        inv = [inv[n] - mm3(*tsp[n], *esp[n]) for n in range(count)]
    states = [jnp.concatenate([eyef, jnp.zeros((DK, DV), f32)], axis=1) for _ in range(2)]
    for c in range(chunks):
        b = c * CH
        kqkq, ktkt = shared[c]
        for e in range(2):
            att, gk, gq, tail, dec, br = per[2 * c + e]
            x = states[e]
            u = mm(kqkq, jnp.concatenate(split(x), axis=0))
            uk = u[:CH] * gk
            vcc = vc[b : b + CH, e * DV : (e + 1) * DV].astype(f32)
            r = jnp.concatenate([-uk[:, :DK], vcc - uk[:, DK:]], axis=1)
            fresh = mm3(*split(inv[2 * c + e] * br), *split(r))
            fh = fresh.astype(bf16)
            o = u[CH:] * gq + mm(att, jnp.concatenate([fh, fh], axis=0))
            reach[b : b + CH, e * DK : (e + 1) * DK] = o[:, :DK]
            loc[b : b + CH, e * DV : (e + 1) * DV] = o[:, DK:]
            states[e] = x * dec + mm(ktkt, jnp.concatenate(split(fresh * tail), axis=0))
    for e in range(2):
        smap[e] = states[e][:, :DK]
        soff[e] = states[e][:, DK:].T


def pass_kernel(maps, rows, entering):
    count = maps.shape[0]

    def step(d, s):
        entering[d] = s
        return nt3(s, maps[d]) + rows[d]

    lax.fori_loop(0, count, step, jnp.zeros(rows.shape[1:], f32))


def out_kernel(loc, reach, state, z, gain, out):
    for e in range(2):
        cols = slice(e * DV, (e + 1) * DV)
        o = loc[:, cols] + nt3(reach[:, cols], state[e])
        ms = jnp.mean(o * o, axis=-1, keepdims=True)
        zf = z[:, cols].astype(f32)
        gated = o * lax.rsqrt(ms + 1e-6) * gain[...] * (zf / (1.0 + jnp.exp(-zf)))
        out[:, cols] = gated.astype(bf16)


def local(q_raw, k_raw, v_raw, conv_weight, gate_log, beta, gate_z, norm_gain, doc_start):
    length = q_raw.shape[0]
    taps = conv_weight.shape[0]
    n = lax.axis_size("ctx")
    pairs = [(i, i + 1) for i in range(n - 1)]
    rims = lax.ppermute(
        (q_raw[length - RIM :], k_raw[length - RIM :], v_raw[length - RIM :]), "ctx", pairs
    )
    chunks = length // CH
    cum = jnp.cumsum(gate_log.reshape(chunks, CH, HV), axis=1).reshape(length, HK, 2)
    bet = beta.reshape(length, HK, 2)
    cumc, cumr = cum.transpose(1, 0, 2), cum.transpose(1, 2, 0)
    betac, betar = bet.transpose(1, 0, 2), bet.transpose(1, 2, 0)
    params = pltpu.CompilerParams(vmem_limit_bytes=50 * 1024 * 1024)
    col1 = lambda rows, off=0: pl.BlockSpec((rows, DK), lambda g, off=off: (0, g + off))
    col2 = lambda rows, off=0: pl.BlockSpec((rows, 2 * DV), lambda g, off=off: (0, g + off))
    cspec = pl.BlockSpec((1, length, 2), lambda g: (g, 0, 0))
    rspec = pl.BlockSpec((1, 2, length), lambda g: (g, 0, 0))
    mspec = pl.BlockSpec((2, DK, DK), lambda g: (g, 0, 0))
    loc, reach, smap, soff = pl.pallas_call(
        slab_kernel,
        grid=(HK,),
        in_specs=[
            pl.BlockSpec(memory_space=pltpu.SMEM),
            col1(length), col1(length), col2(length),
            col1(RIM), col1(RIM), col2(RIM),
            col1(taps), col1(taps, HK), col2(taps, HK),
            cspec, rspec, cspec, rspec,
        ],
        out_specs=[col2(length), col2(length), mspec, mspec],
        out_shape=[
            jax.ShapeDtypeStruct((length, HV * DV), f32),
            jax.ShapeDtypeStruct((length, HV * DK), f32),
            jax.ShapeDtypeStruct((HV, DK, DK), f32),
            jax.ShapeDtypeStruct((HV, DV, DK), f32),
        ],
        scratch_shapes=[pltpu.VMEM((length + RIM, 2 * DV), f32)],
        compiler_params=params,
    )(
        doc_start, q_raw, k_raw, v_raw, *rims, conv_weight, conv_weight, conv_weight,
        cumc, cumr, betac, betar,
    )
    per_head = n // HV
    rc = DV // per_head
    maps_out = jnp.repeat(smap, per_head, axis=0)
    rows_out = soff.reshape(n, rc, DK)
    maps_in = lax.all_to_all(maps_out, "ctx", split_axis=0, concat_axis=0, tiled=True)
    rows_in = lax.all_to_all(rows_out, "ctx", split_axis=0, concat_axis=0, tiled=True)
    entering = pl.pallas_call(
        pass_kernel,
        out_shape=jax.ShapeDtypeStruct((n, rc, DK), f32),
        compiler_params=params,
    )(maps_in, rows_in)
    back = lax.all_to_all(entering, "ctx", split_axis=0, concat_axis=0, tiled=True)
    state = back.reshape(HV, DV, DK)
    return pl.pallas_call(
        out_kernel,
        grid=(HK,),
        in_specs=[
            col2(length), col2(length), mspec, col2(length),
            pl.BlockSpec((1, DV), lambda g: (0, 0)),
        ],
        out_specs=col2(length),
        out_shape=jax.ShapeDtypeStruct((length, HV * DV), bf16),
        compiler_params=params,
    )(loc, reach, state, gate_z, norm_gain.reshape(1, DV))


def solution(mesh):
    rows = P(("groups", "ctx"), None)
    return jax.shard_map(
        local,
        mesh=mesh,
        in_specs=(rows, rows, rows, P(), rows, rows, rows, P(), P(("groups", "ctx"))),
        out_specs=rows,
        check_vma=False,
    )
```

```python
import functools

import jax
import jax.numpy as jnp
from jax import lax
from jax.experimental import pallas as pl
from jax.experimental.pallas import tpu as pltpu
from jax.sharding import PartitionSpec as P

HK = 8
HV = 16
DK = 128
DV = 128
CH = 128
RIM = 16
f32 = jnp.float32
bf16 = jnp.bfloat16


def split(x):
    hi = x.astype(bf16)
    return hi, (x - hi.astype(f32)).astype(bf16)


def mm(a, b):
    return lax.dot_general(a, b, (((1,), (0,)), ((), ())), preferred_element_type=f32)


def mm_nt(a, b):
    return lax.dot_general(a, b, (((1,), (1,)), ((), ())), preferred_element_type=f32)


def mm3(ah, al, bh, bl):
    left = jnp.concatenate([ah, al], axis=1)
    return mm(left, jnp.concatenate([bh, bh], axis=0)) + mm(ah, bl)


def conv(ext, raw, rim, w, since, length):
    width = raw.shape[1]
    ext[0:RIM, 0:width] = rim.astype(f32)
    ext[RIM : RIM + length, 0:width] = raw.astype(f32)
    taps = w.shape[0]
    total = None
    for s in range(taps):
        back = taps - 1 - s
        term = ext[RIM - back : RIM - back + length, 0:width] * w[s : s + 1, :]
        if back:
            term = jnp.where(since < back, 0.0, term)
        total = term if total is None else total + term
    return (total / (1.0 + jnp.exp(-total))).astype(bf16)


def slab(g, doc, q, k, v, rq, rk, rv, wq, wk, wv, cumc, cumr, betac, betar, loc, reach, ext):
    length = q.shape[0]
    one = pl.multiple_of(g * DK, DK)
    two = pl.multiple_of(g * 2 * DV, 2 * DV)
    sd = doc[0]
    row = lax.broadcasted_iota(jnp.int32, (length, DK), 0) - sd
    since = jnp.where(row < 0, length + 8, row)
    qc = conv(ext, q[...], rq[:, pl.ds(one, DK)], wq[...], since, length)
    kc = conv(ext, k[...], rk[:, pl.ds(one, DK)], wk[...], since, length)
    since2 = jnp.concatenate([since, since], axis=1)
    vc = conv(ext, v[...], rv[:, pl.ds(two, 2 * DV)], wv[...], since2, length)
    chunks = length // CH
    ii = lax.broadcasted_iota(jnp.int32, (CH, CH), 0)
    jj = lax.broadcasted_iota(jnp.int32, (CH, CH), 1)
    ix = ii ^ jj
    eye = ii == jj
    eyef = jnp.where(eye, 1.0, 0.0)
    tcol = lax.broadcasted_iota(jnp.int32, (CH, 1), 0)
    shared = []
    lowers = []
    per = []
    for c in range(chunks):
        b = c * CH
        kcc, qcc = kc[b : b + CH], qc[b : b + CH]
        kq = jnp.concatenate([kcc, qcc], axis=0)
        gram = mm_nt(kq, kcc)
        kk = jnp.where(eye, gram[:CH], 0.0)
        k_row = lax.rsqrt(jnp.sum(kk, axis=0, keepdims=True) + 1e-6)
        k_col = lax.rsqrt(jnp.sum(kk, axis=1, keepdims=True) + 1e-6)
        qf = qcc.astype(f32)
        q_col = lax.rsqrt(jnp.sum(qf * qf, axis=1, keepdims=True) + 1e-6) * (DK**-0.5)
        same = (ii + b >= sd) == (jj + b >= sd)
        mask = jnp.where((ii >= jj) & same, 0.0, -1e30)
        gs = gram[:CH] * k_col * k_row
        ats = gram[CH:] * q_col * k_row
        opened = jnp.where((tcol + b >= sd) & (b - 1 < sd), 0.0, 1.0)
        ended = jnp.where((tcol + b < sd) & (b + CH - 1 >= sd), 0.0, 1.0)
        carries = jnp.where((b + CH - 1 >= sd) & (b - 1 < sd), 0.0, 1.0)
        kt = kcc.astype(f32).T.astype(bf16)
        shared.append((jnp.concatenate([kq, kq], axis=1), jnp.concatenate([kt, kt], axis=1)))
        for e in range(2):
            cc = cumc[g, b : b + CH, e : e + 1]
            cr = cumr[g, e : e + 1, b : b + CH]
            bc = betac[g, b : b + CH, e : e + 1]
            br = betar[g, e : e + 1, b : b + CH]
            decay = jnp.exp(cc - cr + mask)
            lower = gs * decay * bc
            att = ats * decay
            growth = jnp.exp(cc) * opened
            last = cc[CH - 1 : CH]
            tail = jnp.exp(last - cc) * ended * k_col
            lowers.append(lower)
            per.append(
                (
                    jnp.concatenate([att.astype(bf16)] * 2, axis=1),
                    growth * k_col,
                    growth * q_col,
                    tail,
                    jnp.exp(last) * carries,
                    br,
                )
            )
    count = len(lowers)
    inv = [eyef - jnp.where(ix == 1, lw, 0.0) for lw in lowers]
    lsp = [split(lw) for lw in lowers]
    for lm in range(1, (CH - 1).bit_length()):
        pick = (ix >> lm) == 1
        zero = jnp.zeros((CH, CH), bf16)
        tsp = [split(t) for t in inv]
        low = [(jnp.where(pick, a, zero), jnp.where(pick, d, zero)) for a, d in lsp]
        es = [mm3(*low[n], *tsp[n]) for n in range(count)]
        esp = [split(x) for x in es]
        inv = [inv[n] - mm3(*tsp[n], *esp[n]) for n in range(count)]
    states = [jnp.concatenate([eyef, jnp.zeros((DK, DV), f32)], axis=1) for _ in range(2)]
    whole = [jnp.ones((1, 1), f32) for _ in range(2)]
    for c in range(chunks):
        b = c * CH
        kqkq, ktkt = shared[c]
        for e in range(2):
            att, gk, gq, tail, dec, br = per[2 * c + e]
            x = states[e]
            u = mm(kqkq, jnp.concatenate(split(x), axis=0))
            uk = u[:CH] * gk
            vcc = vc[b : b + CH, e * DV : (e + 1) * DV].astype(f32)
            r = jnp.concatenate([-uk[:, :DK], vcc - uk[:, DK:]], axis=1)
            fresh = mm3(*split(inv[2 * c + e] * br), *split(r))
            o = u[CH:] * gq + mm(att, jnp.concatenate(split(fresh), axis=0))
            reach[g, b : b + CH, e * DK : (e + 1) * DK] = o[:, :DK].astype(bf16)
            loc[g, b : b + CH, e * DV : (e + 1) * DV] = o[:, DK:]
            whole[e] = whole[e] * dec
            states[e] = x * dec + mm(ktkt, jnp.concatenate(split(fresh * tail), axis=0))
    return states, whole


MAPR = DK + RIM


def prepare(gate, beta, cumc, cumr, betac, betar):
    length = gate.shape[0]
    ii = lax.broadcasted_iota(jnp.int32, (CH, CH), 0)
    jj = lax.broadcasted_iota(jnp.int32, (CH, CH), 1)
    tri = jnp.where(ii >= jj, 1.0, 0.0).astype(bf16)
    pad = jnp.zeros((CH, CH - HV), f32)
    for c in range(length // CH):
        rows = slice(c * CH, (c + 1) * CH)
        x = gate[rows]
        hi, rest = x.astype(bf16), x - x.astype(bf16).astype(f32)
        mid, low = split(rest)
        cum = mm(tri, hi) + mm(tri, mid) + mm(tri, low)
        for val, col, row in ((cum, cumc, cumr), (beta[rows], betac, betar)):
            turned = jnp.concatenate([val, pad], axis=1).T
            for g in range(HK):
                col[g, rows, :] = val[:, 2 * g : 2 * g + 2]
                row[g, :, rows] = turned[2 * g : 2 * g + 2]


def layer_kernel(
    n, doc, q, k, v, wq, wk, wv, gate, beta, z, gain, q_any, k_any, v_any, out,
    rq, rk, rv, cumc, cumr, betac, betar, loc, reach, ext, sbuf, rbuf, ent, inst,
    rim_send, rim_recv, map_send, map_recv, row_send, row_recv, ent_send, ent_recv,
):
    length = q.shape[0]
    t = pl.program_id(0)
    me = lax.axis_index("ctx")
    per_head = n // HV
    rc = DV // per_head
    my_head = me // per_head
    my_row = pl.multiple_of(lax.rem(me, per_head) * rc, rc)

    def remote(src, dst, send, recv, to):
        return pltpu.make_async_remote_copy(
            src_ref=src, dst_ref=dst, send_sem=send, recv_sem=recv,
            device_id={"ctx": to}, device_id_type=pl.DeviceIdType.MESH,
        )

    def rim_copies():
        tail = pl.ds(length - RIM, RIM)
        for i, (a, b) in enumerate(((q_any, rq), (k_any, rk), (v_any, rv))):
            yield remote(a.at[tail], b, rim_send.at[i], rim_recv.at[i], lax.rem(me + 1, n))

    def piece(h, j):
        to = h * per_head + j
        rows = pl.ds(MAPR + j * rc, rc)
        return (
            remote(
                sbuf.at[h, pl.ds(0, MAPR)], rbuf.at[me, pl.ds(0, MAPR)],
                map_send.at[h, j], map_recv.at[me], to,
            ),
            remote(
                sbuf.at[h, rows], rbuf.at[me, pl.ds(MAPR, rc)],
                row_send.at[h, j], row_recv.at[me], to,
            ),
        )

    def arrived(d):
        a, b = pl.ds(0, MAPR), pl.ds(MAPR, rc)
        return (
            remote(sbuf.at[0, a], rbuf.at[d, a], map_send.at[0, 0], map_recv.at[d], d),
            remote(sbuf.at[0, b], rbuf.at[d, b], row_send.at[0, 0], row_recv.at[d], d),
        )

    def entry(d):
        return remote(
            ent.at[d], inst.at[my_head, pl.ds(my_row, rc)], ent_send.at[d], ent_recv.at[me], d
        )

    @pl.when(t == 0)
    def _():
        barrier = pltpu.get_barrier_semaphore()

        def greet(d, _):
            @pl.when(d != me)
            def _():
                pl.semaphore_signal(
                    barrier, inc=1, device_id={"ctx": d}, device_id_type=pl.DeviceIdType.MESH
                )

            return 0

        lax.fori_loop(0, n, greet, 0)
        prepare(gate, beta, cumc, cumr, betac, betar)
        pl.semaphore_wait(barrier, n - 1)

        @pl.when(me < n - 1)
        def _():
            for copy in rim_copies():
                copy.start()

        @pl.when(me == 0)
        def _():
            for r in (rq, rk, rv):
                r[...] = jnp.zeros(r.shape, bf16)

        @pl.when(me > 0)
        def _():
            for copy in rim_copies():
                copy.wait_recv()

        @pl.when(me < n - 1)
        def _():
            for copy in rim_copies():
                copy.wait_send()

    @pl.when(t < HK)
    def _():
        states, whole = slab(
            t, doc, q, k, v, rq, rk, rv, wq, wk, wv, cumc, cumr, betac, betar, loc, reach, ext
        )
        ii = lax.broadcasted_iota(jnp.int32, (DK, DK), 0)
        jj = lax.broadcasted_iota(jnp.int32, (DK, DK), 1)
        ri = lax.broadcasted_iota(jnp.int32, (RIM, DK), 0)
        for e in range(2):
            h = 2 * t + e
            hi = whole[e].astype(bf16).astype(f32)
            mid = (whole[e] - hi).astype(bf16).astype(f32)
            low = whole[e] - hi - mid
            rest = states[e][:, :DK] - jnp.where(ii == jj, whole[e], 0.0)
            facts = jnp.where(ri == 0, hi, jnp.where(ri == 1, mid, jnp.where(ri == 2, low, 0.0)))
            sbuf[h, 0:DK] = rest.astype(bf16)
            sbuf[h, DK:MAPR] = facts.astype(bf16)
            sbuf[h, MAPR : MAPR + DV] = states[e][:, DK:].T.astype(bf16)
            for j in range(per_head):
                @pl.when(h * per_head + j == me)
                def _():
                    rbuf[me, 0:MAPR] = sbuf[h, 0:MAPR]
                    rbuf[me, MAPR : MAPR + rc] = sbuf[h, MAPR + j * rc : MAPR + (j + 1) * rc]

                @pl.when(h * per_head + j != me)
                def _():
                    for copy in piece(h, j):
                        copy.start()

    @pl.when(me // (2 * per_head) == t - LAG)
    def _():
        def step(d, s):
            @pl.when(d != me)
            def _():
                ent[d] = s.astype(bf16)
                entry(d).start()
                for copy in arrived(d):
                    copy.wait_recv()

            @pl.when(d == me)
            def _():
                inst[my_head, pl.ds(my_row, rc)] = s.astype(bf16)

            m = rbuf[d, 0:DK]
            facts = rbuf[d, DK:MAPR].astype(f32)
            decay = jnp.sum(facts, axis=0, keepdims=True)
            moved = mm_nt(jnp.concatenate(split(s), axis=1), jnp.concatenate([m, m], axis=1))
            return s * decay + moved + rbuf[d, MAPR : MAPR + rc].astype(f32)

        lax.fori_loop(0, n, step, jnp.zeros((rc, DK), f32))

    @pl.when(t >= HK)
    def _():
        g = t - HK
        for e in range(2):
            h = 2 * g + e
            for j in range(per_head):
                src = h * per_head + j

                @pl.when(src != me)
                def _():
                    rows = pl.ds(j * rc, rc)
                    remote(
                        ent.at[0], inst.at[h, rows], ent_send.at[0], ent_recv.at[src], src
                    ).wait_recv()

            cols = slice(e * DV, (e + 1) * DV)
            o = loc[g, :, cols] + mm_nt(reach[g, :, cols], inst[h])
            ms = jnp.mean(o * o, axis=-1, keepdims=True)
            zf = z[:, cols].astype(f32)
            gated = o * lax.rsqrt(ms + 1e-6) * gain[...] * (zf / (1.0 + jnp.exp(-zf)))
            out[:, cols] = gated.astype(bf16)

    @pl.when(t == 2 * HK - 1)
    def _():
        def finish(d, _):
            @pl.when(d != me)
            def _():
                entry(d).wait_send()
                for copy in piece(d // per_head, lax.rem(d, per_head)):
                    copy.wait_send()

            return 0

        lax.fori_loop(0, n, finish, 0)


LAG = 2


def local(q_raw, k_raw, v_raw, conv_weight, gate_log, beta, gate_z, norm_gain, doc_start):
    length = q_raw.shape[0]
    taps = conv_weight.shape[0]
    n = lax.axis_size("ctx")
    per_head = n // HV
    rc = DV // per_head
    first = lambda t: jnp.minimum(t, HK - 1)
    second = lambda t: jnp.maximum(t - HK, 0)
    col1 = lambda rows, off=0: pl.BlockSpec((rows, DK), lambda t, off=off: (0, first(t) + off))
    col2 = lambda rows, off=0: pl.BlockSpec((rows, 2 * DV), lambda t, off=off: (0, first(t) + off))
    late = pl.BlockSpec((length, 2 * DV), lambda t: (0, second(t)))
    full = lambda a, b: pl.BlockSpec((a, b), lambda t: (0, 0))
    anywhere = pl.BlockSpec(memory_space=pl.ANY)
    dma = pltpu.SemaphoreType.DMA
    return pl.pallas_call(
        functools.partial(layer_kernel, n),
        grid=(2 * HK,),
        in_specs=[
            pl.BlockSpec(memory_space=pltpu.SMEM),
            col1(length), col1(length), col2(length),
            col1(taps), col1(taps, HK), col2(taps, HK),
            full(length, HV), full(length, HV), late, full(1, DV),
            anywhere, anywhere, anywhere,
        ],
        out_specs=late,
        out_shape=jax.ShapeDtypeStruct((length, HV * DV), bf16),
        scratch_shapes=[
            pltpu.VMEM((RIM, HK * DK), bf16),
            pltpu.VMEM((RIM, HK * DK), bf16),
            pltpu.VMEM((RIM, HV * DV), bf16),
            pltpu.VMEM((HK, length, 2), f32),
            pltpu.VMEM((HK, 2, length), f32),
            pltpu.VMEM((HK, length, 2), f32),
            pltpu.VMEM((HK, 2, length), f32),
            pltpu.VMEM((HK, length, 2 * DV), f32),
            pltpu.VMEM((HK, length, 2 * DK), bf16),
            pltpu.VMEM((length + RIM, 2 * DV), f32),
            pltpu.VMEM((HV, MAPR + DV, DK), bf16),
            pltpu.VMEM((n, MAPR + rc, DK), bf16),
            pltpu.VMEM((n, rc, DK), bf16),
            pltpu.VMEM((HV, DV, DK), bf16),
            dma((3,)), dma((3,)),
            dma((HV, per_head)), dma((n,)),
            dma((HV, per_head)), dma((n,)),
            dma((n,)), dma((n,)),
        ],
        compiler_params=pltpu.CompilerParams(
            vmem_limit_bytes=56 * 1024 * 1024, collective_id=0, has_side_effects=True
        ),
    )(
        doc_start, q_raw, k_raw, v_raw, conv_weight, conv_weight, conv_weight,
        gate_log, beta, gate_z, norm_gain.reshape(1, DV), q_raw, k_raw, v_raw,
    )


def solution(mesh):
    rows = P(("groups", "ctx"), None)
    return jax.shard_map(
        local,
        mesh=mesh,
        in_specs=(rows, rows, rows, P(), rows, rows, rows, P(), P(("groups", "ctx"))),
        out_specs=rows,
        check_vma=False,
    )
```

```python
import functools

import jax
import jax.numpy as jnp
from jax import lax
from jax.experimental import pallas as pl
from jax.experimental.pallas import tpu as pltpu
from jax.sharding import PartitionSpec as P

HK = 8
HV = 16
DK = 128
DV = 128
CH = 128
RIM = 16
f32 = jnp.float32
bf16 = jnp.bfloat16


def split(x):
    hi = x.astype(bf16)
    return hi, (x - hi.astype(f32)).astype(bf16)


def mm(a, b):
    return lax.dot_general(a, b, (((1,), (0,)), ((), ())), preferred_element_type=f32)


def mm_nt(a, b):
    return lax.dot_general(a, b, (((1,), (1,)), ((), ())), preferred_element_type=f32)


def conv(ext, raw, rim, w, since, length):
    width = raw.shape[1]
    ext[0:RIM, 0:width] = rim.astype(f32)
    ext[RIM : RIM + length, 0:width] = raw.astype(f32)
    taps = w.shape[0]
    total = None
    for s in range(taps):
        back = taps - 1 - s
        term = ext[RIM - back : RIM - back + length, 0:width] * w[s : s + 1, :]
        if back:
            term = jnp.where(since < back, 0.0, term)
        total = term if total is None else total + term
    return (total / (1.0 + jnp.exp(-total))).astype(bf16)


def slab(g, doc, q, k, v, rq, rk, rv, wq, wk, wv, cumc, cumr, betac, loc, reach, ext):
    length = q.shape[0]
    one = pl.multiple_of(g * DK, DK)
    two = pl.multiple_of(g * 2 * DV, 2 * DV)
    sd = doc[0]
    row = lax.broadcasted_iota(jnp.int32, (length, DK), 0) - sd
    since = jnp.where(row < 0, length + 8, row)
    qc = conv(ext, q[...], rq[:, pl.ds(one, DK)], wq[...], since, length)
    kc = conv(ext, k[...], rk[:, pl.ds(one, DK)], wk[...], since, length)
    since2 = jnp.concatenate([since, since], axis=1)
    vc = conv(ext, v[...], rv[:, pl.ds(two, 2 * DV)], wv[...], since2, length)
    chunks = length // CH
    ii = lax.broadcasted_iota(jnp.int32, (CH, CH), 0)
    jj = lax.broadcasted_iota(jnp.int32, (CH, CH), 1)
    ix = ii ^ jj
    eye = ii == jj
    eyef = jnp.where(eye, 1.0, 0.0)
    tcol = lax.broadcasted_iota(jnp.int32, (CH, 1), 0)
    shared = []
    lowers = []
    per = []
    for c in range(chunks):
        b = c * CH
        kcc, qcc = kc[b : b + CH], qc[b : b + CH]
        kq = jnp.concatenate([kcc, qcc], axis=0)
        gram = mm_nt(kq, kcc)
        kk = jnp.where(eye, gram[:CH], 0.0)
        k_row = lax.rsqrt(jnp.sum(kk, axis=0, keepdims=True) + 1e-6)
        k_col = lax.rsqrt(jnp.sum(kk, axis=1, keepdims=True) + 1e-6)
        qf = qcc.astype(f32)
        q_col = lax.rsqrt(jnp.sum(qf * qf, axis=1, keepdims=True) + 1e-6) * (DK**-0.5)
        same = (ii + b >= sd) == (jj + b >= sd)
        mask = jnp.where((ii >= jj) & same, 0.0, -1e30)
        gs = gram[:CH] * k_col * k_row
        ats = gram[CH:] * q_col * k_row
        opened = jnp.where((tcol + b >= sd) & (b - 1 < sd), 0.0, 1.0)
        ended = jnp.where((tcol + b < sd) & (b + CH - 1 >= sd), 0.0, 1.0)
        carries = jnp.where((b + CH - 1 >= sd) & (b - 1 < sd), 0.0, 1.0)
        kt = kcc.astype(f32).T.astype(bf16)
        shared.append((jnp.concatenate([kq, kq], axis=1), jnp.concatenate([kt, kt], axis=1)))
        for e in range(2):
            cc = cumc[g, b : b + CH, e : e + 1]
            cr = cumr[g, e : e + 1, b : b + CH]
            bc = betac[g, b : b + CH, e : e + 1]
            decay = jnp.exp(cc - cr + mask)
            lower = gs * decay * bc
            att = ats * decay
            growth = jnp.exp(cc) * opened
            last = cc[CH - 1 : CH]
            tail = jnp.exp(last - cc) * ended * k_col
            lowers.append(lower)
            per.append(
                (
                    jnp.concatenate([att.astype(bf16)] * 2, axis=1),
                    growth * k_col * bc,
                    growth * q_col,
                    tail,
                    jnp.exp(last) * carries,
                    bc,
                )
            )
    count = len(lowers)
    inv = [eyef - jnp.where(ix == 1, lw, 0.0) for lw in lowers]
    lsp = [lw.astype(bf16) for lw in lowers]
    for lm in range(1, (CH - 1).bit_length()):
        pick = (ix >> lm) == 1
        zero = jnp.zeros((CH, CH), bf16)
        tsp = [m.astype(bf16) for m in inv]
        low = [jnp.where(pick, a, zero) for a in lsp]
        es = [mm(low[n], tsp[n]).astype(bf16) for n in range(count)]
        inv = [inv[n] - mm(tsp[n], es[n]) for n in range(count)]
    states = [jnp.concatenate([eyef, jnp.zeros((DK, DV), f32)], axis=1) for _ in range(2)]
    tts = [jnp.concatenate([m.astype(bf16)] * 2, axis=1) for m in inv]
    whole = [jnp.ones((1, 1), f32) for _ in range(2)]
    for c in range(chunks):
        b = c * CH
        kqkq, ktkt = shared[c]
        pair = per[2 * c : 2 * c + 2]
        us = [mm(kqkq, jnp.concatenate(split(x), axis=0)) for x in states]
        rs = []
        for e in range(2):
            uk = us[e][:CH] * pair[e][1]
            vcc = vc[b : b + CH, e * DV : (e + 1) * DV].astype(f32) * pair[e][5]
            rs.append(jnp.concatenate([-uk[:, :DK], vcc - uk[:, DK:]], axis=1))
        fresh = [
            mm(tts[2 * c + e], jnp.concatenate(split(rs[e]), axis=0)) for e in range(2)
        ]
        for e in range(2):
            states[e] = states[e] * pair[e][4] + mm(
                ktkt, jnp.concatenate(split(fresh[e] * pair[e][3]), axis=0)
            )
            whole[e] = whole[e] * pair[e][4]
        for e in range(2):
            o = us[e][CH:] * pair[e][2] + mm(pair[e][0], jnp.concatenate(split(fresh[e]), axis=0))
            reach[g, b : b + CH, e * DK : (e + 1) * DK] = o[:, :DK].astype(bf16)
            loc[g, b : b + CH, e * DV : (e + 1) * DV] = o[:, DK:]
    return states, whole


MAPR = DK + RIM


def prepare(gate, beta, cumc, cumr, betac):
    length = gate.shape[0]
    ii = lax.broadcasted_iota(jnp.int32, (CH, CH), 0)
    jj = lax.broadcasted_iota(jnp.int32, (CH, CH), 1)
    tri = jnp.where(ii >= jj, 1.0, 0.0).astype(bf16)
    pad = jnp.zeros((CH, CH - HV), f32)
    for c in range(length // CH):
        rows = slice(c * CH, (c + 1) * CH)
        x = gate[rows]
        hi, rest = x.astype(bf16), x - x.astype(bf16).astype(f32)
        mid, low = split(rest)
        cum = mm(tri, hi) + mm(tri, mid) + mm(tri, low)
        turned = jnp.concatenate([cum, pad], axis=1).T
        for g in range(HK):
            cumc[g, rows, :] = cum[:, 2 * g : 2 * g + 2]
            cumr[g, :, rows] = turned[2 * g : 2 * g + 2]
            betac[g, rows, :] = beta[rows, 2 * g : 2 * g + 2]


def layer_kernel(
    n, doc, q, k, v, wq, wk, wv, gate, beta, z, gain, q_any, k_any, v_any, out,
    rq, rk, rv, cumc, cumr, betac, loc, reach, ext, sbuf, rbuf, ent, inst,
    rim_send, rim_recv, map_send, map_recv, row_send, row_recv, ent_send, ent_recv,
):
    length = q.shape[0]
    t = pl.program_id(0)
    me = lax.axis_index("ctx")
    per_head = n // HV
    rc = DV // per_head
    my_head = me // per_head
    my_row = pl.multiple_of(lax.rem(me, per_head) * rc, rc)

    def remote(src, dst, send, recv, to):
        return pltpu.make_async_remote_copy(
            src_ref=src, dst_ref=dst, send_sem=send, recv_sem=recv,
            device_id={"ctx": to}, device_id_type=pl.DeviceIdType.MESH,
        )

    def rim_copies():
        tail = pl.ds(length - RIM, RIM)
        for i, (a, b) in enumerate(((q_any, rq), (k_any, rk), (v_any, rv))):
            yield remote(a.at[tail], b, rim_send.at[i], rim_recv.at[i], lax.rem(me + 1, n))

    def piece(h, j):
        to = h * per_head + j
        rows = pl.ds(MAPR + j * rc, rc)
        return (
            remote(
                sbuf.at[h, pl.ds(0, MAPR)], rbuf.at[me, pl.ds(0, MAPR)],
                map_send.at[h, j], map_recv.at[me], to,
            ),
            remote(
                sbuf.at[h, rows], rbuf.at[me, pl.ds(MAPR, rc)],
                row_send.at[h, j], row_recv.at[me], to,
            ),
        )

    def arrived(d):
        a, b = pl.ds(0, MAPR), pl.ds(MAPR, rc)
        return (
            remote(sbuf.at[0, a], rbuf.at[d, a], map_send.at[0, 0], map_recv.at[d], d),
            remote(sbuf.at[0, b], rbuf.at[d, b], row_send.at[0, 0], row_recv.at[d], d),
        )

    def entry(d):
        return remote(
            ent.at[d], inst.at[my_head, pl.ds(my_row, rc)], ent_send.at[d], ent_recv.at[me], d
        )

    @pl.when(t == 0)
    def _():
        barrier = pltpu.get_barrier_semaphore()

        def greet(d, _):
            @pl.when(d != me)
            def _():
                pl.semaphore_signal(
                    barrier, inc=1, device_id={"ctx": d}, device_id_type=pl.DeviceIdType.MESH
                )

            return 0

        lax.fori_loop(0, n, greet, 0)
        prepare(gate, beta, cumc, cumr, betac)
        pl.semaphore_wait(barrier, n - 1)

        @pl.when(me < n - 1)
        def _():
            for copy in rim_copies():
                copy.start()

        @pl.when(me == 0)
        def _():
            for r in (rq, rk, rv):
                r[...] = jnp.zeros(r.shape, bf16)

        @pl.when(me > 0)
        def _():
            for copy in rim_copies():
                copy.wait_recv()

        @pl.when(me < n - 1)
        def _():
            for copy in rim_copies():
                copy.wait_send()

    @pl.when(t < HK)
    def _():
        states, whole = slab(
            t, doc, q, k, v, rq, rk, rv, wq, wk, wv, cumc, cumr, betac, loc, reach, ext
        )
        ii = lax.broadcasted_iota(jnp.int32, (DK, DK), 0)
        jj = lax.broadcasted_iota(jnp.int32, (DK, DK), 1)
        ri = lax.broadcasted_iota(jnp.int32, (RIM, DK), 0)
        for e in range(2):
            h = 2 * t + e
            hi = whole[e].astype(bf16).astype(f32)
            mid = (whole[e] - hi).astype(bf16).astype(f32)
            low = whole[e] - hi - mid
            rest = states[e][:, :DK] - jnp.where(ii == jj, whole[e], 0.0)
            facts = jnp.where(ri == 0, hi, jnp.where(ri == 1, mid, jnp.where(ri == 2, low, 0.0)))
            sbuf[h, 0:DK] = rest.astype(bf16)
            sbuf[h, DK:MAPR] = facts.astype(bf16)
            sbuf[h, MAPR : MAPR + DV] = states[e][:, DK:].T.astype(bf16)
            for j in range(per_head):
                @pl.when(h * per_head + j == me)
                def _():
                    rbuf[me, 0:MAPR] = sbuf[h, 0:MAPR]
                    rbuf[me, MAPR : MAPR + rc] = sbuf[h, MAPR + j * rc : MAPR + (j + 1) * rc]

                @pl.when(h * per_head + j != me)
                def _():
                    for copy in piece(h, j):
                        copy.start()

    @pl.when(me // (2 * per_head) == t - LAG)
    def _():
        def step(d, s):
            @pl.when(d != me)
            def _():
                ent[d] = s.astype(bf16)
                entry(d).start()
                for copy in arrived(d):
                    copy.wait_recv()

            @pl.when(d == me)
            def _():
                inst[my_head, pl.ds(my_row, rc)] = s.astype(bf16)

            m = rbuf[d, 0:DK]
            facts = rbuf[d, DK:MAPR].astype(f32)
            decay = jnp.sum(facts, axis=0, keepdims=True)
            moved = mm_nt(jnp.concatenate(split(s), axis=1), jnp.concatenate([m, m], axis=1))
            return s * decay + moved + rbuf[d, MAPR : MAPR + rc].astype(f32)

        lax.fori_loop(0, n, step, jnp.zeros((rc, DK), f32))

    @pl.when(t >= HK)
    def _():
        g = t - HK
        for e in range(2):
            h = 2 * g + e
            for j in range(per_head):
                src = h * per_head + j

                @pl.when(src != me)
                def _():
                    rows = pl.ds(j * rc, rc)
                    remote(
                        ent.at[0], inst.at[h, rows], ent_send.at[0], ent_recv.at[src], src
                    ).wait_recv()

            cols = slice(e * DV, (e + 1) * DV)
            o = loc[g, :, cols] + mm_nt(reach[g, :, cols], inst[h])
            ms = jnp.mean(o * o, axis=-1, keepdims=True)
            zf = z[:, cols].astype(f32)
            gated = o * lax.rsqrt(ms + 1e-6) * gain[...] * (zf / (1.0 + jnp.exp(-zf)))
            out[:, cols] = gated.astype(bf16)

    @pl.when(t == 2 * HK - 1)
    def _():
        def finish(d, _):
            @pl.when(d != me)
            def _():
                entry(d).wait_send()
                for copy in piece(d // per_head, lax.rem(d, per_head)):
                    copy.wait_send()

            return 0

        lax.fori_loop(0, n, finish, 0)


LAG = 2


def local(q_raw, k_raw, v_raw, conv_weight, gate_log, beta, gate_z, norm_gain, doc_start):
    length = q_raw.shape[0]
    taps = conv_weight.shape[0]
    n = lax.axis_size("ctx")
    per_head = n // HV
    rc = DV // per_head
    first = lambda t: jnp.minimum(t, HK - 1)
    second = lambda t: jnp.maximum(t - HK, 0)
    col1 = lambda rows, off=0: pl.BlockSpec((rows, DK), lambda t, off=off: (0, first(t) + off))
    col2 = lambda rows, off=0: pl.BlockSpec((rows, 2 * DV), lambda t, off=off: (0, first(t) + off))
    late = pl.BlockSpec((length, 2 * DV), lambda t: (0, second(t)))
    full = lambda a, b: pl.BlockSpec((a, b), lambda t: (0, 0))
    anywhere = pl.BlockSpec(memory_space=pl.ANY)
    dma = pltpu.SemaphoreType.DMA
    return pl.pallas_call(
        functools.partial(layer_kernel, n),
        grid=(2 * HK,),
        in_specs=[
            pl.BlockSpec(memory_space=pltpu.SMEM),
            col1(length), col1(length), col2(length),
            col1(taps), col1(taps, HK), col2(taps, HK),
            full(length, HV), full(length, HV), late, full(1, DV),
            anywhere, anywhere, anywhere,
        ],
        out_specs=late,
        out_shape=jax.ShapeDtypeStruct((length, HV * DV), bf16),
        scratch_shapes=[
            pltpu.VMEM((RIM, HK * DK), bf16),
            pltpu.VMEM((RIM, HK * DK), bf16),
            pltpu.VMEM((RIM, HV * DV), bf16),
            pltpu.VMEM((HK, length, 2), f32),
            pltpu.VMEM((HK, 2, length), f32),
            pltpu.VMEM((HK, length, 2), f32),
            pltpu.VMEM((HK, length, 2 * DV), f32),
            pltpu.VMEM((HK, length, 2 * DK), bf16),
            pltpu.VMEM((length + RIM, 2 * DV), f32),
            pltpu.VMEM((HV, MAPR + DV, DK), bf16),
            pltpu.VMEM((n, MAPR + rc, DK), bf16),
            pltpu.VMEM((n, rc, DK), bf16),
            pltpu.VMEM((HV, DV, DK), bf16),
            dma((3,)), dma((3,)),
            dma((HV, per_head)), dma((n,)),
            dma((HV, per_head)), dma((n,)),
            dma((n,)), dma((n,)),
        ],
        compiler_params=pltpu.CompilerParams(
            vmem_limit_bytes=56 * 1024 * 1024, collective_id=0, has_side_effects=True
        ),
    )(
        doc_start, q_raw, k_raw, v_raw, conv_weight, conv_weight, conv_weight,
        gate_log, beta, gate_z, norm_gain.reshape(1, DV), q_raw, k_raw, v_raw,
    )


def solution(mesh):
    rows = P(("groups", "ctx"), None)
    return jax.shard_map(
        local,
        mesh=mesh,
        in_specs=(rows, rows, rows, P(), rows, rows, rows, P(), P(("groups", "ctx"))),
        out_specs=rows,
        check_vma=False,
    )
```
